256 devices in a mesh: fit: 32 (over x, y, core), batch: 8 (over z).
Axes of the slice: x: 4, y: 4, z: 8, core: 2. Of those that a mesh axis runs over, the one named last changes fastest.
Arguments:
- half_ints: bfloat16 [30720, 384, 128], P('fit', 'batch')
- domain_tiles: int32 [256, 6], P('batch'), may hold values from 0 to 7, as said below
- tile_counts: int32 [256, 6], P('batch'), may hold values from 0 to 128, as said below
Outputs:
- exchange_k: float32 [1024, 1024], P('fit', 'batch')
The draws below stay inside these ranges and needn't reach their ends.
Inputs may be any that keep to these rules, and one draw needn't show every extreme that they name: `tile_counts`: in each orbital the slots with a count above 0 come first. In every group of 32 orbitals there are 48 such slots: exactly one orbital has 6, 11 others have 2, the rest 1, so that the squared numbers sum to 100. Every live slot but an orbital's last holds 128 valid functions. `domain_tiles`: the tiles of one orbital differ.
All inputs are finite; a program needn't handle non-finite values.
Results may differ from the reference program's by a relative error of at most 0.0003.
Values sent between devices are 32-bit elements; how exact they have to be, the bound alone decides.
No kernel may reach another device: no remote copies, remote signals or barrier semaphores. Data moves between devices by JAX's collectives and lax.ppermute only.
A program may use at most 192 MiB of HBM per device.

```python
import math
import jax
import jax.numpy as jnp
from jax import lax

TILE = 128
MAXT = 6
TILES = 8
NAUX = 30720
ORB_G = 32
ORB_ALL = 256
SLOTS = 48
SLOTS_ALL = 384
NB = 1024
N_BATCH = 8


def draw_tile_counts(key, part):
    key = jax.random.fold_in(key, 11)
    rank_key, last_key = jax.random.split(key)
    keys = jax.random.split(rank_key, N_BATCH)
    ranks = jax.vmap(lambda k: jax.random.permutation(k, ORB_G))(keys).reshape(-1)
    doubles = SLOTS - ORB_G - MAXT + 1
    live_count = jnp.where(ranks == 0, MAXT, jnp.where(ranks <= doubles, 2, 1))
    last = jax.random.randint(last_key, (ORB_ALL,), 1, 129)
    within = jnp.arange(MAXT)[None, :]
    counts = jnp.where(within < live_count[:, None] - 1, 128, jnp.where(within == live_count[:, None] - 1, last[:, None], 0))
    return counts.astype(jnp.int32)


def draw_domain_tiles(key, part):
    key = jax.random.fold_in(key, 12)
    keys = jax.random.split(key, ORB_ALL)
    chosen = jax.vmap(lambda k: jax.random.permutation(k, TILES)[:MAXT])(keys)
    return chosen.astype(jnp.int32)


def draw_half_ints(key, part):
    key = jax.random.fold_in(key, 13)
    value_key = jax.random.fold_in(key, 0)
    common_key = jax.random.fold_in(key, 2)
    coeff_key = jax.random.fold_in(key, 3)
    values = jax.random.normal(value_key, (NAUX, SLOTS_ALL, TILE), jnp.float32)
    common = jax.random.normal(common_key, (NAUX, 1, 1), jnp.float32)
    coeff = jax.random.normal(coeff_key, (1, SLOTS_ALL, TILE), jnp.float32)
    mixed = values + 0.7 * jnp.roll(values, 1, axis=2) + 2.0 * common * coeff
    return (mixed * (0.15 / math.sqrt(NAUX))).astype(jnp.bfloat16)


def setup_inputs(seed: int = 0) -> dict:
    key_list = jax.random.split(jax.random.key(seed), 4)
    return {
        "half_ints": draw_half_ints(jax.random.fold_in(key_list[3], 71), 0),
        "domain_tiles": draw_domain_tiles(jax.random.fold_in(key_list[3], 71), 0),
        "tile_counts": draw_tile_counts(jax.random.fold_in(key_list[3], 71), 0),
    }


def pair_lists(counts, slots):
    orbitals = counts.shape[0]
    widest = counts.shape[1]
    pairs_total = widest * widest + orbitals - 1 + 3 * (slots - orbitals - widest + 1)
    live_count = jnp.sum((counts > 0).astype(jnp.int32), axis=1, dtype=jnp.int32)
    offset = (jnp.cumsum(live_count, dtype=jnp.int32) - live_count).astype(jnp.int32)
    within = jnp.arange(widest, dtype=jnp.int32)
    column = (offset[:, None] + within[None, :]).astype(jnp.int32)
    live = within[None, :] < live_count[:, None]
    target = jnp.where(live, column, slots).astype(jnp.int32)
    slot_count = jnp.zeros((slots,), jnp.int32).at[target.reshape(-1)].set(counts.reshape(-1), mode="drop")
    valid = (live[:, :, None] & live[:, None, :]).reshape(-1)
    left_col = jnp.broadcast_to(column[:, :, None], (orbitals, widest, widest)).reshape(-1)
    right_col = jnp.broadcast_to(column[:, None, :], (orbitals, widest, widest)).reshape(-1)
    position = (jnp.cumsum(valid.astype(jnp.int32), dtype=jnp.int32) - 1).astype(jnp.int32)
    place_at = jnp.where(valid, position, pairs_total).astype(jnp.int32)
    left_list = jnp.zeros((pairs_total,), jnp.int32).at[place_at].set(left_col, mode="drop")
    right_list = jnp.zeros((pairs_total,), jnp.int32).at[place_at].set(right_col, mode="drop")
    return slot_count, left_list, right_list, place_at


def tile_lists(tiles, place_at, pairs_total):
    orbitals = tiles.shape[0]
    widest = tiles.shape[1]
    row_flat = jnp.broadcast_to(tiles[:, :, None], (orbitals, widest, widest)).reshape(-1)
    col_flat = jnp.broadcast_to(tiles[:, None, :], (orbitals, widest, widest)).reshape(-1)
    row_tiles = jnp.zeros((pairs_total,), jnp.int32).at[place_at].set(row_flat, mode="drop")
    col_tiles = jnp.zeros((pairs_total,), jnp.int32).at[place_at].set(col_flat, mode="drop")
    return row_tiles, col_tiles


def mask_blocks(blocks, slot_count):
    inside = jnp.arange(blocks.shape[2], dtype=jnp.int32)[None, None, :] < slot_count[None, :, None]
    return jnp.where(inside, blocks, jnp.zeros_like(blocks))


def place(grams, row_tiles, col_tiles, tile_total):
    width = grams.shape[1]
    blocks = jnp.zeros((tile_total, tile_total, width, width), jnp.float32).at[row_tiles, col_tiles].add(grams)
    return blocks.transpose(0, 2, 1, 3).reshape(tile_total * width, tile_total * width)


def reference(half_ints, domain_tiles, tile_counts):
    total = jnp.zeros((NB, NB), jnp.float32)
    for group in range(N_BATCH):
        blocks = half_ints[:, group * SLOTS:(group + 1) * SLOTS, :]
        counts = tile_counts[group * ORB_G:(group + 1) * ORB_G]
        tiles = domain_tiles[group * ORB_G:(group + 1) * ORB_G]
        slot_count, left_list, right_list, place_at = pair_lists(counts, SLOTS)
        row_tiles, col_tiles = tile_lists(tiles, place_at, left_list.shape[0])
        masked = mask_blocks(blocks, slot_count)

        def one_gram(index):
            left = lax.dynamic_index_in_dim(masked, left_list[index], 1, keepdims=False)
            right = lax.dynamic_index_in_dim(masked, right_list[index], 1, keepdims=False)
            return jnp.dot(left.T, right, preferred_element_type=jnp.float32)

        grams = lax.map(one_gram, jnp.arange(left_list.shape[0], dtype=jnp.int32))
        total = total + place(grams, row_tiles, col_tiles, TILES)
    return total
```

```python
import jax
import jax.numpy as jnp
import numpy as np
from jax import lax
from jax.experimental import pallas as pl
from jax.experimental.pallas import tpu as pltpu
from jax.sharding import PartitionSpec as P

TILE = 128
TILES = 8
HALF = TILES // 2
MAXT = 6
ORBITALS = 32
SLOTS = 48
DOUBLES = 11
SINGLES = 20
CHUNKS = 10
CORES = 2
SET = 20


def stored_index():
    table = np.zeros((CORES, TILES, TILES), np.int32)
    where = {}
    for half in range(2):
        for a in range(HALF):
            for b in range(a, HALF):
                where[half * HALF + a, half * HALF + b] = (0, len(where))
    for a in range(HALF):
        for b in range(HALF):
            where[a, HALF + b] = (1, a * HALF + b)
    for (a, b), (owner, index) in where.items():
        for core in range(CORES):
            table[core, a, b] = (owner ^ core) * SET + index
    return table, where


TABLE, PLACES = stored_index()


def tn_dot(a, b):
    return lax.dot_general(a, b, (((0,), (0,)), ((), ())), preferred_element_type=jnp.float32)


def gram_kernel(
    table_ref, tiles_ref, counts_ref, x_hbm, keep_hbm, send_hbm,
    raw, slots, acc, mask, slot_count, ones, twos, six, load_sem, out_sem,
):
    rows = raw.shape[0] // CHUNKS
    core = lax.rem(lax.axis_index("fit"), CORES)

    def load(i):
        part = pl.ds(i * rows, rows)
        return pltpu.make_async_copy(x_hbm.at[part], raw.at[part], load_sem.at[i])

    for i in range(CHUNKS):
        load(i).start()

    acc[...] = jnp.zeros_like(acc)

    def place(a, b):
        return table_ref[core * (TILES * TILES) + jnp.minimum(a, b) * TILES + jnp.maximum(a, b)]

    def orbital(i, carry):
        offset, n_one, n_two = carry
        live = jnp.int32(0)
        for k in range(MAXT):
            count = counts_ref[i, k]
            slot_count[offset + k] = count
            live = live + (count > 0).astype(jnp.int32)
        first, second = tiles_ref[i, 0], tiles_ref[i, 1]
        ones[0, n_one] = offset
        ones[1, n_one] = place(first, first)
        swap = (first > second).astype(jnp.int32)
        low, high = jnp.minimum(first, second), jnp.maximum(first, second)
        twos[0, n_two] = offset + swap
        twos[1, n_two] = offset + 1 - swap
        twos[2, n_two] = place(low, low)
        twos[3, n_two] = place(low, high)
        twos[4, n_two] = place(high, high)

        @pl.when(live == MAXT)
        def _():
            for k in range(MAXT):
                rank = jnp.int32(0)
                for l in range(MAXT):
                    if l != k:
                        rank = rank + (tiles_ref[i, l] < tiles_ref[i, k]).astype(jnp.int32)
                six[0, rank] = offset + k
                six[1, rank] = tiles_ref[i, k]

        return (
            offset + live,
            n_one + (live == 1).astype(jnp.int32),
            n_two + (live == 2).astype(jnp.int32),
        )

    zero = jnp.int32(0)
    lax.fori_loop(0, ORBITALS, orbital, (zero, zero, zero))

    lane = lax.broadcasted_iota(jnp.int32, (1, TILE), 1)
    for s in range(SLOTS):
        mask[s] = (lane < slot_count[s]).astype(jnp.float32).astype(jnp.bfloat16)

    for i in range(CHUNKS):
        load(i).wait()
        part = pl.ds(i * rows, rows)
        slots[:, part, :] = jnp.swapaxes(raw[part], 0, 1) * mask[...]

    def side(columns):
        return jnp.concatenate([slots[c] for c in columns], axis=1)

    order = [six[0, k] for k in range(MAXT)]
    tile_of = [six[1, k] for k in range(MAXT)]
    for pair in range(MAXT // 2):
        right = side(order[2 * pair:2 * pair + 2])
        gram = tn_dot(side(order[:2 * pair + 2]), right)
        for a in range(2 * pair + 2):
            for b in range(2):
                if a <= 2 * pair + b:
                    acc[place(tile_of[a], tile_of[2 * pair + b])] += gram[
                        a * TILE:(a + 1) * TILE, b * TILE:(b + 1) * TILE
                    ]
    for j in range(DOUBLES):
        both = side([twos[0, j], twos[1, j]])
        gram = tn_dot(both, both)
        acc[twos[2, j]] += gram[:TILE, :TILE]
        acc[twos[3, j]] += gram[:TILE, TILE:]
        acc[twos[4, j]] += gram[TILE:, TILE:]
    for j in range(SINGLES):
        only = slots[ones[0, j]]
        acc[ones[1, j]] += tn_dot(only, only)

    keep = pltpu.make_async_copy(acc.at[pl.ds(0, SET)], keep_hbm, out_sem.at[0])
    send = pltpu.make_async_copy(acc.at[pl.ds(SET, SET)], send_hbm, out_sem.at[1])
    keep.start()
    send.start()
    keep.wait()
    send.wait()


def grams(half_ints, domain_tiles, tile_counts):
    fit_rows = half_ints.shape[0]
    half = jax.ShapeDtypeStruct((SET, TILE, TILE), jnp.float32)
    smem = pl.BlockSpec(memory_space=pltpu.SMEM)
    return pl.pallas_call(
        gram_kernel,
        in_specs=[smem, smem, smem, pl.BlockSpec(memory_space=pl.ANY)],
        out_specs=[pl.BlockSpec(memory_space=pl.ANY)] * 2,
        out_shape=[half, half],
        scratch_shapes=[
            pltpu.VMEM((fit_rows, SLOTS, TILE), jnp.bfloat16),
            pltpu.VMEM((SLOTS, fit_rows, TILE), jnp.bfloat16),
            pltpu.VMEM((CORES * SET, TILE, TILE), jnp.float32),
            pltpu.VMEM((SLOTS, 1, TILE), jnp.bfloat16),
            pltpu.SMEM((SLOTS + MAXT,), jnp.int32),
            pltpu.SMEM((2, ORBITALS), jnp.int32),
            pltpu.SMEM((5, ORBITALS), jnp.int32),
            pltpu.SMEM((2, MAXT), jnp.int32),
            pltpu.SemaphoreType.DMA((CHUNKS,)),
            pltpu.SemaphoreType.DMA((2,)),
        ],
        compiler_params=pltpu.CompilerParams(vmem_limit_bytes=48 * 2**20),
        name="grams",
    )(jnp.asarray(TABLE.reshape(-1)), domain_tiles, tile_counts, half_ints)


def expand_kernel(keep_ref, other_ref, out_ref):
    core = lax.rem(lax.axis_index("fit"), CORES)
    strip = TILE // 4

    def put(row, col, block):
        m = col % HALF
        for q in range(4):
            out_ref[row * 4 + q, m * strip:(m + 1) * strip, :] = block[q * strip:(q + 1) * strip]

    for owner in range(CORES):
        @pl.when(core == owner)
        def _():
            for (a, b), (held_by, index) in PLACES.items():
                if held_by == owner:
                    block = keep_ref[index] + other_ref[index]
                    put(a, b, block)
                    if a != b:
                        put(b, a, block.T)


def expand(keep, other):
    vmem = pl.BlockSpec(memory_space=pltpu.VMEM)
    return pl.pallas_call(
        expand_kernel,
        in_specs=[vmem, vmem],
        out_specs=vmem,
        out_shape=jax.ShapeDtypeStruct((32, TILE, TILE), jnp.float32),
        compiler_params=pltpu.CompilerParams(vmem_limit_bytes=48 * 2**20),
        name="expand",
    )(keep, other)


def local(half_ints, domain_tiles, tile_counts):
    keep, send = grams(half_ints, domain_tiles, tile_counts)
    swap = [(f, f ^ 1) for f in range(32)]
    other = lax.ppermute(send, "fit", swap)
    strips = expand(keep, other)
    parts = lax.all_to_all(strips, "fit", 0, 0)
    row = jnp.sum(parts.reshape(16, CORES, HALF * 32, TILE), axis=0)
    upper = lax.axis_index("fit") >= 16
    row = jnp.where(upper, row[::-1], row).reshape(TILES, 32, TILE)
    blocks = lax.all_to_all(row, "batch", 0, 0)
    return jnp.sum(blocks, axis=0)


def solution(mesh):
    return jax.shard_map(
        local,
        mesh=mesh,
        in_specs=(P("fit", "batch", None), P("batch", None), P("batch", None)),
        out_specs=P("fit", "batch"),
        check_vma=False,
    )
```

```python
import jax
import jax.numpy as jnp
from jax import lax
from jax.experimental import pallas as pl
from jax.experimental.pallas import tpu as pltpu
from jax.sharding import PartitionSpec as P

TILE = 128
TILES = 8
MAXT = 6
ORBITALS = 32
SLOTS = 48
DOUBLES = 11
SINGLES = 20
CHUNKS = 10
CORES = 2
HALF = TILE // 2
BLOCKS = TILES + 1
PIECE = 16
ROW_CHIPS = 2 * TILES


def tn_dot(a, b):
    return lax.dot_general(a, b, (((0,), (0,)), ((), ())), preferred_element_type=jnp.float32)


def left_lanes(shape):
    return lax.broadcasted_iota(jnp.int32, shape, len(shape) - 1) < HALF


def gram_kernel(
    tiles_ref, counts_ref, x_hbm, keep_ref, send_ref,
    raw, slots, acc, mask, slot_count, ones, twos, six, load_sem,
):
    rows = raw.shape[0] // CHUNKS
    core = lax.rem(lax.axis_index("fit"), CORES)

    def load(i):
        part = pl.ds(i * rows, rows)
        return pltpu.make_async_copy(x_hbm.at[part], raw.at[part], load_sem.at[i])

    for i in range(CHUNKS):
        load(i).start()

    acc[...] = jnp.zeros_like(acc)

    def orbital(i, carry):
        offset, n_one, n_two = carry
        live = jnp.int32(0)
        for k in range(MAXT):
            count = counts_ref[k, i]
            slot_count[offset + k] = count
            live = live + (count > 0).astype(jnp.int32)
        first, second = tiles_ref[0, i], tiles_ref[1, i]
        ones[0, n_one] = offset
        ones[1, n_one] = first
        swap = (first > second).astype(jnp.int32)
        twos[0, n_two] = offset + swap
        twos[1, n_two] = offset + 1 - swap
        twos[2, n_two] = jnp.minimum(first, second)
        twos[3, n_two] = jnp.maximum(first, second)

        @pl.when(live == MAXT)
        def _():
            for k in range(MAXT):
                rank = jnp.int32(0)
                for l in range(MAXT):
                    if l != k:
                        rank = rank + (tiles_ref[l, i] < tiles_ref[k, i]).astype(jnp.int32)
                six[0, rank] = offset + k
                six[1, rank] = tiles_ref[k, i]

        return (
            offset + live,
            n_one + (live == 1).astype(jnp.int32),
            n_two + (live == 2).astype(jnp.int32),
        )

    zero = jnp.int32(0)
    lax.fori_loop(0, ORBITALS, orbital, (zero, zero, zero))

    lane = lax.broadcasted_iota(jnp.int32, (1, TILE), 1)
    for s in range(SLOTS):
        mask[s] = (lane < slot_count[s]).astype(jnp.float32).astype(jnp.bfloat16)

    for i in range(CHUNKS):
        load(i).wait()
        part = pl.ds(i * rows, rows)
        slots[:, part, :] = jnp.swapaxes(raw[part], 0, 1) * mask[...]

    def side(columns):
        return jnp.concatenate([slots[c] for c in columns], axis=1)

    left = left_lanes((HALF, TILE))

    def even(gram):
        return jnp.where(left, gram[:HALF], gram[HALF:])

    def odd(gram):
        return jnp.where(left, gram[HALF:], gram[:HALF])

    def add(a, b, gram, order):
        if order <= 0:
            acc[a * BLOCKS + b] += even(gram)
        if order > 0:
            acc[a * BLOCKS + b] += odd(gram)
        if order == 0:
            acc[a * BLOCKS + TILES] += odd(gram)

    order = [six[0, k] for k in range(MAXT)]
    tile_of = [six[1, k] for k in range(MAXT)]
    left_side = side(order)
    for pair in range(MAXT // 2):
        gram = tn_dot(left_side, side(order[2 * pair:2 * pair + 2]))
        for a in range(MAXT):
            for b in (2 * pair, 2 * pair + 1):
                block = gram[a * TILE:(a + 1) * TILE, (b - 2 * pair) * TILE:(b - 2 * pair + 1) * TILE]
                add(tile_of[a], tile_of[b], block, a - b)
    for j in range(DOUBLES):
        both = side([twos[0, j], twos[1, j]])
        gram = tn_dot(both, both)
        low, high = twos[2, j], twos[3, j]
        add(low, low, gram[:TILE, :TILE], 0)
        add(low, high, gram[:TILE, TILE:], -1)
        add(high, low, gram[TILE:, :TILE], 1)
        add(high, high, gram[TILE:, TILE:], 0)
    for j in range(SINGLES):
        only = slots[ones[0, j]]
        add(ones[1, j], ones[1, j], tn_dot(only, only), 0)

    near = left_lanes((PIECE, TILE))
    for target, part in ((send_ref, 1 - core), (keep_ref, core)):
        start = pl.multiple_of(part * 2 * PIECE, 2 * PIECE)
        for a in range(TILES):
            for b in range(BLOCKS):
                block = acc[a * BLOCKS + b, pl.ds(start, 2 * PIECE), :]
                top, bottom = block[:PIECE], block[PIECE:]
                first = jnp.where(near, top, pltpu.roll(bottom, HALF, 1))
                second = jnp.where(near, pltpu.roll(top, HALF, 1), bottom)
                if b < a or b == TILES:
                    first, second = second, first
                target[2 * a, b * PIECE:(b + 1) * PIECE, :] = first
                target[2 * a + 1, b * PIECE:(b + 1) * PIECE, :] = second


def grams(half_ints, domain_tiles, tile_counts):
    fit_rows = half_ints.shape[0]
    half = jax.ShapeDtypeStruct((ROW_CHIPS, BLOCKS * PIECE, TILE), jnp.float32)
    smem = pl.BlockSpec(memory_space=pltpu.SMEM)
    vmem = pl.BlockSpec(memory_space=pltpu.VMEM)
    return pl.pallas_call(
        gram_kernel,
        in_specs=[smem, smem, pl.BlockSpec(memory_space=pl.ANY)],
        out_specs=[vmem, vmem],
        out_shape=[half, half],
        scratch_shapes=[
            pltpu.VMEM((fit_rows, SLOTS, TILE), jnp.bfloat16),
            pltpu.VMEM((SLOTS, fit_rows, TILE), jnp.bfloat16),
            pltpu.VMEM((TILES * BLOCKS, HALF, TILE), jnp.float32),
            pltpu.VMEM((SLOTS, 1, TILE), jnp.bfloat16),
            pltpu.SMEM((SLOTS + MAXT,), jnp.int32),
            pltpu.SMEM((2, ORBITALS), jnp.int32),
            pltpu.SMEM((4, ORBITALS), jnp.int32),
            pltpu.SMEM((2, MAXT), jnp.int32),
            pltpu.SemaphoreType.DMA((CHUNKS,)),
        ],
        compiler_params=pltpu.CompilerParams(vmem_limit_bytes=48 * 2**20),
        name="grams",
    )(domain_tiles.T, tile_counts.T, half_ints)


def assemble_kernel(mine_ref, same_ref, cross_ref, out_ref):
    fit = lax.axis_index("fit")
    core = lax.rem(fit, CORES)
    row = fit // 4
    half = lax.rem(fit // 2, 2)
    col = lax.axis_index("batch")
    near = left_lanes((PIECE, TILE))

    def unpack(piece):
        moved = pltpu.roll(piece, HALF, 1)
        return jnp.concatenate([jnp.where(near, piece, moved), jnp.where(near, moved, piece)], axis=0)

    own = unpack(mine_ref[:PIECE])
    extra = unpack(mine_ref[PIECE:])
    same, cross = unpack(same_ref[...]), unpack(cross_ref[...])
    low = jnp.where(core == 0, same, cross)
    high = jnp.where(core == 0, cross, same)
    block = jnp.concatenate([low, high], axis=0)
    flipped = jnp.concatenate([block, block], axis=0).T
    received = jnp.where(core == 0, flipped[:2 * PIECE], flipped[2 * PIECE:4 * PIECE])
    other = jnp.where(row == col, extra, received)
    own_half = jnp.where(row <= col, half, 1 - half)
    lane_half = lax.broadcasted_iota(jnp.int32, (2 * PIECE, TILE), 1) // HALF
    out_ref[...] = jnp.where(lane_half == own_half, own, other)


def assemble(mine, same, cross):
    vmem = pl.BlockSpec(memory_space=pltpu.VMEM)
    return pl.pallas_call(
        assemble_kernel,
        in_specs=[vmem] * 3,
        out_specs=vmem,
        out_shape=jax.ShapeDtypeStruct((2 * PIECE, TILE), jnp.float32),
        name="assemble",
    )(mine, same, cross)


def mirror_moves():
    same, cross = [], []
    for row in range(TILES):
        for half in range(2):
            for core in range(CORES):
                for col in range(TILES):
                    there = half if row < col else 1 - half
                    source = ((row * 2 + half) * CORES + core) * TILES + col
                    for moves, to_core in ((same, core), (cross, 1 - core)):
                        moves.append((source, ((col * 2 + there) * CORES + to_core) * TILES + row))
    return same, cross


def local(half_ints, domain_tiles, tile_counts):
    keep, send = grams(half_ints, domain_tiles, tile_counts)
    other = lax.ppermute(send, "fit", [(f, f ^ 1) for f in range(2 * ROW_CHIPS)])
    chip = keep + other
    same_core = [[CORES * p + core for p in range(ROW_CHIPS)] for core in range(CORES)]
    parts = lax.all_to_all(chip, "fit", 0, 0, axis_index_groups=same_core)
    row = jnp.sum(parts, axis=0).reshape(BLOCKS, PIECE, TILE)
    extra = jnp.broadcast_to(row[TILES:], (TILES, PIECE, TILE))
    blocks = lax.all_to_all(jnp.concatenate([row[:TILES], extra], axis=1), "batch", 0, 0)
    mine = jnp.sum(blocks, axis=0)
    same_moves, cross_moves = mirror_moves()
    own = mine[:PIECE]
    same = lax.ppermute(own, ("fit", "batch"), same_moves)
    cross = lax.ppermute(own, ("fit", "batch"), cross_moves)
    return assemble(mine, same, cross)


def solution(mesh):
    return jax.shard_map(
        local,
        mesh=mesh,
        in_specs=(P("fit", "batch", None), P("batch", None), P("batch", None)),
        out_specs=P("fit", "batch"),
        check_vma=False,
    )
```

```python
import jax
import jax.numpy as jnp
from jax import lax
from jax.experimental import pallas as pl
from jax.experimental.pallas import tpu as pltpu
from jax.sharding import PartitionSpec as P

TILE = 128
TILES = 8
MAXT = 6
ORBITALS = 32
SLOTS = 48
DOUBLES = 11
SINGLES = 20
CHUNKS = 15
CORES = 2
RING = 4
STRIP = 32
STRIPS = TILE // STRIP
CHIPS = RING * RING
FORWARD, BACKWARD, JOINED, OWN = range(4)


def tn_dot(a, b):
    return lax.dot_general(a, b, (((0,), (0,)), ((), ())), preferred_element_type=jnp.float32)


def place():
    fit = lax.axis_index("fit")
    return fit // (RING * CORES), lax.rem(fit // CORES, RING), lax.rem(fit, CORES)


def gram_kernel(
    tiles_hbm, counts_hbm, x_hbm, out_ref,
    raw, slots, ones, twos, six, row_base, tiles_ref, counts_ref, load_sem, index_sem,
):
    rows = raw.shape[0] // CHUNKS

    def load(i):
        part = pl.ds(i * rows, rows)
        return pltpu.make_async_copy(x_hbm.at[part], raw.at[part], load_sem.at[i])

    load_tiles = pltpu.make_async_copy(tiles_hbm, tiles_ref, index_sem.at[0])
    load_counts = pltpu.make_async_copy(counts_hbm, counts_ref, index_sem.at[1])
    load_tiles.start()
    load_counts.start()
    for i in range(CHUNKS):
        load(i).start()
    out_ref[...] = jnp.zeros_like(out_ref)

    x, y, core = place()
    for a in range(TILES):
        for q in range(STRIPS):
            to_x, to_y = a // 2, (a % 2) * 2 + q // 2
            u, w = ((to_y - y) & (RING - 1), to_x) if q % 2 == 0 else ((to_x - x) & (RING - 1), to_y)
            by_step = (OWN, JOINED, FORWARD, BACKWARD) if w < RING // 2 else (OWN, FORWARD, BACKWARD, JOINED)
            leg = jnp.int32(by_step[0])
            for step in range(1, RING):
                leg = jnp.where(u == step, by_step[step], leg)
            row_base[a, q] = (((q % 2) ^ core) * CHIPS + leg * RING + w) * TILES

    load_tiles.wait()
    load_counts.wait()

    offset = n_one = n_two = six_at = six_offset = jnp.int32(0)
    for i in range(ORBITALS):
        last = counts_ref[1, i]
        more = (last > 0).astype(jnp.int32)
        many = (counts_ref[2, i] > 0).astype(jnp.int32)
        first, second = tiles_ref[0, i], tiles_ref[1, i]
        ones[0, n_one] = offset
        ones[1, n_one] = first
        ones[2, n_one] = counts_ref[0, i]
        ordered = first < second
        twos[0, n_two] = jnp.where(ordered, offset, offset + 1)
        twos[1, n_two] = jnp.where(ordered, offset + 1, offset)
        twos[2, n_two] = jnp.where(ordered, first, second)
        twos[3, n_two] = jnp.where(ordered, second, first)
        twos[4, n_two] = jnp.where(ordered, TILE, last)
        twos[5, n_two] = jnp.where(ordered, last, TILE)
        six_at = six_at + many * i
        six_offset = six_offset + many * offset
        offset = offset + 1 + more + (MAXT - 2) * many
        n_one = n_one + 1 - more
        n_two = n_two + more - many
    for k in range(MAXT):
        rank = jnp.int32(0)
        for l in range(MAXT):
            if l != k:
                rank = rank + (tiles_ref[l, six_at] < tiles_ref[k, six_at]).astype(jnp.int32)
        six[0, rank] = six_offset + k
        six[1, rank] = tiles_ref[k, six_at]
        six[2, rank] = counts_ref[k, six_at]

    for i in range(CHUNKS):
        load(i).wait()
        part = pl.ds(i * rows, rows)
        slots[:, part, :] = jnp.swapaxes(raw[part], 0, 1)

    lane = lax.broadcasted_iota(jnp.int32, (1, TILE), 1)

    def masked(column, count):
        return slots[column] * (lane < count).astype(jnp.float32).astype(jnp.bfloat16)

    def add(a, b, gram):
        for q in range(STRIPS):
            out_ref[row_base[a, q] + b] += gram[q * STRIP:(q + 1) * STRIP]

    tile_of = [six[1, k] for k in range(MAXT)]
    sides = [masked(six[0, k], six[2, k]) for k in range(MAXT)]
    left_side = jnp.concatenate(sides, axis=1)
    for pair in range(MAXT // 2):
        gram = tn_dot(left_side, jnp.concatenate(sides[2 * pair:2 * pair + 2], axis=1))
        for a in range(MAXT):
            for b in (2 * pair, 2 * pair + 1):
                block = gram[a * TILE:(a + 1) * TILE, (b - 2 * pair) * TILE:(b - 2 * pair + 1) * TILE]
                add(tile_of[a], tile_of[b], block)
    for j in range(DOUBLES):
        both = jnp.concatenate([masked(twos[0, j], twos[4, j]), masked(twos[1, j], twos[5, j])], axis=1)
        gram = tn_dot(both, both)
        low, high = twos[2, j], twos[3, j]
        add(low, low, gram[:TILE, :TILE])
        add(low, high, gram[:TILE, TILE:])
        add(high, low, gram[TILE:, :TILE])
        add(high, high, gram[TILE:, TILE:])
    for j in range(SINGLES):
        only = masked(ones[0, j], ones[2, j])
        add(ones[1, j], ones[1, j], tn_dot(only, only))


def grams(half_ints, domain_tiles, tile_counts):
    fit_rows = half_ints.shape[0]
    hbm = pl.BlockSpec(memory_space=pltpu.HBM)
    return pl.pallas_call(
        gram_kernel,
        in_specs=[hbm, hbm, pl.BlockSpec(memory_space=pl.ANY)],
        out_specs=pl.BlockSpec(memory_space=pltpu.VMEM),
        out_shape=jax.ShapeDtypeStruct((CORES * CHIPS * TILES, STRIP, TILE), jnp.float32),
        scratch_shapes=[
            pltpu.VMEM((fit_rows, SLOTS, TILE), jnp.bfloat16),
            pltpu.VMEM((SLOTS, fit_rows, TILE), jnp.bfloat16),
            pltpu.SMEM((3, ORBITALS), jnp.int32),
            pltpu.SMEM((6, ORBITALS), jnp.int32),
            pltpu.SMEM((3, MAXT), jnp.int32),
            pltpu.SMEM((TILES, STRIPS), jnp.int32),
            pltpu.SMEM((MAXT, ORBITALS), jnp.int32),
            pltpu.SMEM((MAXT, ORBITALS), jnp.int32),
            pltpu.SemaphoreType.DMA((CHUNKS,)),
            pltpu.SemaphoreType.DMA((2,)),
        ],
        compiler_params=pltpu.CompilerParams(vmem_limit_bytes=48 * 2**20),
        name="grams",
    )(domain_tiles.T, tile_counts.T, half_ints)


def ring_moves(step, turn):
    moves = []
    for x in range(RING):
        for y in range(RING):
            for core in range(CORES):
                along_x = core != turn
                to_x = (x + step) % RING if along_x else x
                to_y = y if along_x else (y + step) % RING
                moves.append(((x * RING + y) * CORES + core, (to_x * RING + to_y) * CORES + core))
    return moves


def first_ring(parts):
    keep, send = parts[0], parts[1]
    swap = [(f, f ^ 1) for f in range(CHIPS * CORES)]
    forward, backward, joined, own = (
        keep[leg] + lax.ppermute(send[leg], "fit", swap) for leg in range(4)
    )
    half = RING // 2
    on = lax.ppermute(forward, "fit", ring_moves(1, 0))
    back = lax.ppermute(backward, "fit", ring_moves(-1, 0))
    joined_on = lax.ppermute(joined[:half] + on[:half], "fit", ring_moves(1, 0))
    joined_back = lax.ppermute(joined[half:] + back[half:], "fit", ring_moves(-1, 0))
    return jnp.concatenate(
        [own[:half] + back[:half] + joined_on, own[half:] + on[half:] + joined_back], axis=0
    )


def second_groups():
    groups = []
    for core in range(CORES):
        for fixed in range(RING):
            groups.append([])
            for moving in range(RING):
                x, y = (moving, fixed) if core == 0 else (fixed, moving)
                fit = (x * RING + y) * CORES + core
                groups[-1] += [fit * TILES + z for z in range(TILES)]
    return groups


def local(half_ints, domain_tiles, tile_counts):
    parts = grams(half_ints, domain_tiles, tile_counts)
    line = first_ring(parts.reshape(CORES, RING, RING, TILES * STRIP, TILE))
    line = line.reshape(RING * TILES, STRIP, TILE)
    strips = lax.all_to_all(line, ("fit", "batch"), 0, 0, axis_index_groups=second_groups())
    return jnp.sum(strips, axis=0)


def solution(mesh):
    return jax.shard_map(
        local,
        mesh=mesh,
        in_specs=(P("fit", "batch", None), P("batch", None), P("batch", None)),
        out_specs=P("fit", "batch"),
        check_vma=False,
    )
```

```python
import jax
import jax.numpy as jnp
from jax import lax
from jax.experimental import pallas as pl
from jax.experimental.pallas import tpu as pltpu
from jax.sharding import PartitionSpec as P

TILE = 128
TILES = 8
MAXT = 6
ORBITALS = 32
SLOTS = 48
DOUBLES = 11
SINGLES = 20
CHUNKS = 15
CORES = 2
RING = 4
HALF = TILE // 2
STRIP = 32
BLOCKS = 16
DIAGONALS = TILES // 2
EIGHT = EXTRA = 8
SHARE = BLOCKS * STRIP + EXTRA


def tn_dot(a, b):
    return lax.dot_general(a, b, (((0,), (0,)), ((), ())), preferred_element_type=jnp.float32)


def left_lanes(shape):
    return lax.broadcasted_iota(jnp.int32, shape, len(shape) - 1) < HALF


def same_index(low, high, odd):
    if isinstance(odd, int):
        m, n = low >> 1, high >> 1
        if odd:
            return (n * 4 + m) if low & 1 else (m * 4 + n)
        return 12 + m if m == n else (low & 1) * 6 + m * 3 - m * (m - 1) // 2 + n - m - 1
    m, n = low >> 1, high >> 1
    mixed = jnp.where((low & 1) == 1, n * 4 + m, m * 4 + n)
    alike = (low & 1) * 6 + m * 3 - ((m * (m - 1)) >> 1) + n - m - 1
    return jnp.where(odd == 1, mixed, jnp.where(m == n, 12 + m, alike))


def cross_pair(k, index):
    if k == 0:
        m = index % 4
        return (2 * m, 2 * m + 1) if index < 4 else (2 * m, 2 * m)
    m = [m for m in range(RING) if m < m ^ k][index // 4]
    return 2 * m + (index // 2) % 2, 2 * (m ^ k) + index % 2


def place():
    fit = lax.axis_index("fit")
    return fit // (RING * CORES), lax.rem(fit // CORES, RING), lax.rem(fit, CORES)


def gram_kernel(
    slots_hbm, x_hbm, out_ref,
    raw, slots, same, cross, ones, twos, six, legs, slots_ref, load_sem, index_sem,
):
    rows = raw.shape[0] // CHUNKS

    def load(i):
        part = pl.ds(i * rows, rows)
        return pltpu.make_async_copy(x_hbm.at[part], raw.at[part], load_sem.at[i])

    load_slots = pltpu.make_async_copy(slots_hbm, slots_ref, index_sem)
    load_slots.start()
    for i in range(CHUNKS):
        load(i).start()
    same[...] = jnp.zeros_like(same)
    cross[...] = jnp.zeros_like(cross)
    out_ref[...] = jnp.zeros_like(out_ref)

    x, y, core = place()
    for owner, here in enumerate((y, x)):
        for there in range(RING):
            legs[owner * RING + there] = ((owner ^ core) * RING + ((there - here) & (RING - 1))) * (SHARE // EIGHT)

    load_slots.wait()

    def tile(k, i):
        return slots_ref[k, i] >> 8

    def count(k, i):
        return slots_ref[k, i] & 255

    offset = n_one = n_two = six_at = six_offset = jnp.int32(0)
    for i in range(ORBITALS):
        last = count(1, i)
        more = (last > 0).astype(jnp.int32)
        many = (count(2, i) > 0).astype(jnp.int32)
        first, second = tile(0, i), tile(1, i)
        ones[0, n_one] = offset
        ones[1, n_one] = first
        ones[2, n_one] = count(0, i)
        ordered = first < second
        twos[0, n_two] = jnp.where(ordered, offset, offset + 1)
        twos[1, n_two] = jnp.where(ordered, offset + 1, offset)
        twos[2, n_two] = jnp.where(ordered, first, second)
        twos[3, n_two] = jnp.where(ordered, second, first)
        twos[4, n_two] = jnp.where(ordered, TILE, last)
        twos[5, n_two] = jnp.where(ordered, last, TILE)
        six_at = six_at + many * i
        six_offset = six_offset + many * offset
        offset = offset + 1 + more + (MAXT - 2) * many
        n_one = n_one + 1 - more
        n_two = n_two + more - many
    for k in range(MAXT):
        rank = jnp.int32(0)
        for l in range(MAXT):
            if l != k:
                rank = rank + (tile(l, six_at) < tile(k, six_at)).astype(jnp.int32)
        six[0, rank] = six_offset + k
        six[1, rank] = tile(k, six_at)
        six[2, rank] = count(k, six_at)

    for i in range(CHUNKS):
        load(i).wait()
        part = pl.ds(i * rows, rows)
        slots[:, part, :] = jnp.swapaxes(raw[part], 0, 1)

    lane = lax.broadcasted_iota(jnp.int32, (1, TILE), 1)

    def masked(column, count):
        return slots[column] * (lane < count).astype(jnp.float32).astype(jnp.bfloat16)

    left = left_lanes((HALF, TILE))

    def add(a, b, gram):
        pair = a * TILES + b
        same[pair] += jnp.where(left, gram[:HALF], gram[HALF:])
        cross[pair] += jnp.where(left, gram[HALF:], gram[:HALF])

    tile_of = [six[1, k] for k in range(MAXT)]
    sides = [masked(six[0, k], six[2, k]) for k in range(MAXT)]
    for pair in range(MAXT // 2):
        gram = tn_dot(jnp.concatenate(sides[:2 * pair + 2], axis=1), jnp.concatenate(sides[2 * pair:2 * pair + 2], axis=1))
        for b in (2 * pair, 2 * pair + 1):
            for a in range(b + 1):
                block = gram[a * TILE:(a + 1) * TILE, (b - 2 * pair) * TILE:(b - 2 * pair + 1) * TILE]
                add(tile_of[a], tile_of[b], block)
    for j in range(DOUBLES):
        both = jnp.concatenate([masked(twos[0, j], twos[4, j]), masked(twos[1, j], twos[5, j])], axis=1)
        gram = tn_dot(both, both)
        low, high = twos[2, j], twos[3, j]
        add(low, low, gram[:TILE, :TILE])
        add(low, high, gram[:TILE, TILE:])
        add(high, high, gram[TILE:, TILE:])
    for j in range(SINGLES):
        only = masked(ones[0, j], ones[2, j])
        add(ones[1, j], ones[1, j], tn_dot(only, only))

    z = lax.axis_index("batch")
    near = left_lanes((STRIP, TILE))
    row_of = lax.broadcasted_iota(jnp.int32, (HALF, TILE), 0)
    col_of = lax.broadcasted_iota(jnp.int32, (HALF, TILE), 1) & (HALF - 1)
    for a in range(TILES):
        for b in range(a, TILES):
            block = same[a * TILES + b]
            if a == b and a % 2 == 1:
                continue
            if a == b:
                beside = same[(a + 1) * (TILES + 1)]
                block = jnp.where(row_of >= col_of, block, beside)
                diagonal = jnp.sum(jnp.where(row_of == col_of, beside, 0.0), axis=0, keepdims=True)
                for i in range(2):
                    out_ref[legs[(z & 1) * 2 + i] + BLOCKS * STRIP // EIGHT, a // 2:a // 2 + 1, :] = diagonal
            top, bottom = block[:STRIP], block[STRIP:]
            first = jnp.where(near, top, pltpu.roll(bottom, HALF, 1))
            second = jnp.where(near, pltpu.roll(top, HALF, 1), bottom)
            odd = (a ^ b) & 1
            index = same_index(a, b, odd)
            for i, value in enumerate((first, second)):
                to_y = ((z & 1) ^ odd) * 2 + i
                rows = pl.ds(legs[to_y] + index * (STRIP // EIGHT), STRIP // EIGHT)
                out_ref[rows] = value.reshape(STRIP // EIGHT, EIGHT, TILE)
    for k in range(RING):
        target = legs[RING + (k ^ (z >> 1))]
        for index in range(TILES):
            a, b = cross_pair(k, index)
            if a == b:
                value = jnp.where(left, cross[(a + 1) * (TILES + 1)], cross[a * (TILES + 1)])
            else:
                value = cross[a * TILES + b]
            rows = pl.ds(target + index * (HALF // EIGHT), HALF // EIGHT)
            out_ref[rows] = value.reshape(HALF // EIGHT, EIGHT, TILE)


def grams(half_ints, domain_tiles, tile_counts):
    fit_rows = half_ints.shape[0]
    hbm = pl.BlockSpec(memory_space=pltpu.HBM)
    return pl.pallas_call(
        gram_kernel,
        in_specs=[hbm, pl.BlockSpec(memory_space=pl.ANY)],
        out_specs=pl.BlockSpec(memory_space=pltpu.VMEM),
        out_shape=jax.ShapeDtypeStruct((CORES * RING * SHARE // EIGHT, EIGHT, TILE), jnp.float32),
        scratch_shapes=[
            pltpu.VMEM((fit_rows, SLOTS, TILE), jnp.bfloat16),
            pltpu.VMEM((SLOTS, fit_rows, TILE), jnp.bfloat16),
            pltpu.VMEM((TILES * TILES, HALF, TILE), jnp.float32),
            pltpu.VMEM((TILES * TILES, HALF, TILE), jnp.float32),
            pltpu.SMEM((3, ORBITALS), jnp.int32),
            pltpu.SMEM((6, ORBITALS), jnp.int32),
            pltpu.SMEM((3, MAXT), jnp.int32),
            pltpu.SMEM((CORES * RING,), jnp.int32),
            pltpu.SMEM((MAXT, ORBITALS), jnp.int32),
            pltpu.SemaphoreType.DMA((CHUNKS,)),
            pltpu.SemaphoreType.DMA,
        ],
        compiler_params=pltpu.CompilerParams(vmem_limit_bytes=48 * 2**20),
        name="grams",
    )((domain_tiles * 256 + tile_counts).T, half_ints)


def ring_moves(step, turn):
    moves = []
    for x in range(RING):
        for y in range(RING):
            for core in range(CORES):
                along_x = core != turn
                to_x = (x + step) % RING if along_x else x
                to_y = y if along_x else (y + step) % RING
                moves.append(((x * RING + y) * CORES + core, (to_x * RING + to_y) * CORES + core))
    return moves


def expand_kernel(own_ref, one_ref, two_ref, three_ref, out_ref, line, blocks):
    line[...] = own_ref[...] + one_ref[...] + two_ref[...] + three_ref[...]
    x, y, core = place()
    z = lax.axis_index("batch")
    near = left_lanes((STRIP, TILE))

    def pack(pair):
        top, bottom = pair[:STRIP], pair[STRIP:]
        return (
            jnp.where(near, top, pltpu.roll(bottom, HALF, 1)),
            jnp.where(near, pltpu.roll(top, HALF, 1), bottom),
        )

    def keep_flipped(pairs, indices):
        turned = jnp.concatenate(pairs, axis=0).T
        flipped = (*pack(turned[:HALF]), *pack(turned[HALF:]))
        for index, value in zip(indices, flipped):
            blocks[BLOCKS + index] = value

    @pl.when(core == 0)
    def _():
        packed = [line[n * STRIP:(n + 1) * STRIP] for n in range(BLOCKS)]
        for n in range(BLOCKS):
            blocks[n] = packed[n]
        pairs = []
        for n in range(0, BLOCKS, 2):
            a, b = packed[n], packed[n + 1]
            top = jnp.where(near, a, pltpu.roll(b, HALF, 1))
            bottom = jnp.where(near, pltpu.roll(a, HALF, 1), b)
            pairs.append(jnp.concatenate([top, bottom], axis=0))
        for n in range(0, BLOCKS, 4):
            keep_flipped(pairs[n // 2:n // 2 + 2], (n, n + 2, n + 1, n + 3))
        odd = (y >> 1) ^ (z & 1)
        row_of = lax.broadcasted_iota(jnp.int32, (STRIP, TILE), 0)
        lane_of = lax.broadcasted_iota(jnp.int32, (STRIP, TILE), 1)
        row_of = row_of + (lane_of // HALF) * STRIP
        col_of = lane_of & (HALF - 1)
        diagonals = line[BLOCKS * STRIP:]
        on_half = (lax.broadcasted_iota(jnp.int32, (EXTRA, TILE), 1) // HALF) == (y & 1)
        diagonals = jnp.where(on_half, diagonals, pltpu.roll(diagonals, HALF, 1))

        @pl.when(odd == 0)
        def _():
            for m in range(DIAGONALS):
                both, turned = blocks[12 + m], blocks[BLOCKS + 12 + m]
                second = jnp.where(row_of < col_of, both, turned)
                blocks[12 + m] = jnp.where(row_of >= col_of, both, turned)
                blocks[BLOCKS + 12 + m] = jnp.where(row_of == col_of, diagonals[m:m + 1], second)

        for to_x in range(RING):
            for col in range(TILES):
                row = 2 * to_x + ((col & 1) ^ odd)
                index = same_index(jnp.minimum(row, col), jnp.maximum(row, col), odd)
                flip = jnp.where(row == col, (row & 1) == 1, row > col)
                out_ref[((to_x - x) & (RING - 1)) * TILES + col] = blocks[jnp.where(flip, index + BLOCKS, index)]

    @pl.when(core == 1)
    def _():
        pairs = [line[n * HALF:(n + 1) * HALF] for n in range(TILES)]
        for n in range(TILES):
            blocks[2 * n], blocks[2 * n + 1] = pack(pairs[n])
        for n in range(0, TILES, 2):
            keep_flipped(pairs[n:n + 2], (2 * n, 2 * n + 2, 2 * n + 1, 2 * n + 3))
        k = x ^ (z >> 1)
        for to_y in range(RING):
            for col in range(TILES):
                row = 2 * ((col >> 1) ^ k) + (to_y >> 1)
                i = to_y & 1
                low, high = jnp.minimum(row, col), jnp.maximum(row, col)
                m = low >> 1
                index = jnp.where(k == 1, m >> 1, m) * 4 + (low & 1) * 2 + (high & 1)
                index = jnp.where(k == 0, jnp.where(row == col, 4 + m, m), index)
                lower_half = jnp.where(row == col, row & 1, jnp.where(row < col, i, 1 - i))
                direct = jnp.where(row == col, (row & 1) == i, row < col)
                index = index * 2 + 1 - lower_half
                out_ref[((to_y - y) & (RING - 1)) * TILES + col] = blocks[jnp.where(direct, index, index + BLOCKS)]


def expand(*pieces):
    vmem = pl.BlockSpec(memory_space=pltpu.VMEM)
    return pl.pallas_call(
        expand_kernel,
        in_specs=[vmem] * len(pieces),
        out_specs=vmem,
        out_shape=jax.ShapeDtypeStruct((RING * TILES, STRIP, TILE), jnp.float32),
        scratch_shapes=[
            pltpu.VMEM((SHARE, TILE), jnp.float32),
            pltpu.VMEM((2 * BLOCKS, STRIP, TILE), jnp.float32),
        ],
        compiler_params=pltpu.CompilerParams(vmem_limit_bytes=8 * 2**20),
        name="expand",
    )(*pieces)


def last_groups():
    groups = []
    for x in range(RING):
        for odd in range(2):
            for i in range(2):
                groups.append([
                    ((x * RING + ((z & 1) ^ odd) * 2 + i) * CORES) * TILES + z for z in range(TILES)
                ])
    for k in range(RING):
        for y in range(RING):
            groups.append([
                ((((z >> 1) ^ k) * RING + y) * CORES + 1) * TILES + z for z in range(TILES)
            ])
    return groups


def local(half_ints, domain_tiles, tile_counts):
    parts = grams(half_ints, domain_tiles, tile_counts).reshape(CORES, RING, SHARE, TILE)
    keep, send = parts[0], parts[1]
    swap = [(f, f ^ 1) for f in range(RING * RING * CORES)]
    chip = {u: keep[u] + lax.ppermute(send[u], "fit", swap) for u in (2, 1, 3, 0)}
    moved = [lax.ppermute(chip[u], "fit", ring_moves(u, 0)) for u in (2, 1, 3)]
    fit = lax.axis_index("fit")
    core = fit & 1
    column_half = ((fit >> 1) & 1) ^ core
    line = expand(chip[0], *moved).reshape(RING, TILES, STRIP, TILE)
    row = line[0]
    for w in (2, 1, 3):
        row = row + lax.ppermute(line[w], "fit", ring_moves(w, 1))
    row, core, column_half = lax.optimization_barrier((row, core, column_half))
    terms = lax.all_to_all(row, ("fit", "batch"), 0, 0, axis_index_groups=last_groups())
    terms, core, column_half = lax.optimization_barrier((terms, core, column_half))
    mine = jnp.sum(terms, axis=0)
    other = lax.ppermute(mine, "fit", swap)
    at = jnp.arange(TILE, dtype=jnp.int32)[None, :] // HALF
    turned_mine, turned_other = (jnp.roll(block, HALF, axis=1) for block in (mine, other))
    return jnp.where(
        at == column_half,
        jnp.where(core == column_half, mine, turned_mine),
        jnp.where(core == column_half, turned_other, other),
    )


def solution(mesh):
    return jax.shard_map(
        local,
        mesh=mesh,
        in_specs=(P("fit", "batch", None), P("batch", None), P("batch", None)),
        out_specs=P("fit", "batch"),
        check_vma=False,
    )
```

```python
import jax
import jax.numpy as jnp
from jax import lax
from jax.experimental import pallas as pl
from jax.experimental.pallas import tpu as pltpu
from jax.sharding import PartitionSpec as P

TILE = 128
TILES = 8
MAXT = 6
ORBITALS = 32
SLOTS = 48
DOUBLES = 11
SINGLES = 20
CHUNKS = 15
CORES = 2
RING = 4
HALF = TILE // 2
STRIP = 32
BLOCKS = 16
DIAGONALS = TILES // 2
EIGHT = EXTRA = 8
SHARE = BLOCKS * STRIP + EXTRA


def tn_dot(a, b):
    return lax.dot_general(a, b, (((0,), (0,)), ((), ())), preferred_element_type=jnp.float32)


def left_lanes(shape):
    return lax.broadcasted_iota(jnp.int32, shape, len(shape) - 1) < HALF


def same_index(low, high, odd):
    if isinstance(odd, int):
        m, n = low >> 1, high >> 1
        if odd:
            return (n * 4 + m) if low & 1 else (m * 4 + n)
        return 12 + m if m == n else (low & 1) * 6 + m * 3 - m * (m - 1) // 2 + n - m - 1
    m, n = low >> 1, high >> 1
    mixed = jnp.where((low & 1) == 1, n * 4 + m, m * 4 + n)
    alike = (low & 1) * 6 + m * 3 - ((m * (m - 1)) >> 1) + n - m - 1
    return jnp.where(odd == 1, mixed, jnp.where(m == n, 12 + m, alike))


def cross_pair(k, index):
    if k == 0:
        m = index % 4
        return (2 * m, 2 * m + 1) if index < 4 else (2 * m, 2 * m)
    m = [m for m in range(RING) if m < m ^ k][index // 4]
    return 2 * m + (index // 2) % 2, 2 * (m ^ k) + index % 2


def place():
    fit = lax.axis_index("fit")
    return fit // (RING * CORES), lax.rem(fit // CORES, RING), lax.rem(fit, CORES)


def gram_kernel(
    slots_hbm, x_hbm, out_ref,
    raw, slots, same, cross, ones, twos, six, legs, slots_ref, load_sem, index_sem,
):
    rows = raw.shape[0] // CHUNKS

    def load(i):
        part = pl.ds(i * rows, rows)
        return pltpu.make_async_copy(x_hbm.at[part], raw.at[part], load_sem.at[i])

    load_slots = pltpu.make_async_copy(slots_hbm, slots_ref, index_sem)
    load_slots.start()
    for i in range(CHUNKS):
        load(i).start()
    same[...] = jnp.zeros_like(same)
    cross[...] = jnp.zeros_like(cross)
    out_ref[...] = jnp.zeros_like(out_ref)

    x, y, core = place()
    for owner, here in enumerate((y, x)):
        for there in range(RING):
            legs[owner * RING + there] = ((owner ^ core) * RING + ((there - here) & (RING - 1))) * (SHARE // EIGHT)

    load_slots.wait()

    def tile(k, i):
        return slots_ref[k, i] >> 8

    def count(k, i):
        return slots_ref[k, i] & 255

    offset = n_one = n_two = six_at = six_offset = jnp.int32(0)
    for i in range(ORBITALS):
        last = count(1, i)
        more = (last > 0).astype(jnp.int32)
        many = (count(2, i) > 0).astype(jnp.int32)
        first, second = tile(0, i), tile(1, i)
        ones[0, n_one] = offset
        ones[1, n_one] = first
        ones[2, n_one] = count(0, i)
        ordered = first < second
        twos[0, n_two] = jnp.where(ordered, offset, offset + 1)
        twos[1, n_two] = jnp.where(ordered, offset + 1, offset)
        twos[2, n_two] = jnp.where(ordered, first, second)
        twos[3, n_two] = jnp.where(ordered, second, first)
        twos[4, n_two] = jnp.where(ordered, TILE, last)
        twos[5, n_two] = jnp.where(ordered, last, TILE)
        six_at = six_at + many * i
        six_offset = six_offset + many * offset
        offset = offset + 1 + more + (MAXT - 2) * many
        n_one = n_one + 1 - more
        n_two = n_two + more - many
    for k in range(MAXT):
        rank = jnp.int32(0)
        for l in range(MAXT):
            if l != k:
                rank = rank + (tile(l, six_at) < tile(k, six_at)).astype(jnp.int32)
        six[0, rank] = six_offset + k
        six[1, rank] = tile(k, six_at)
        six[2, rank] = count(k, six_at)

    for i in range(CHUNKS):
        load(i).wait()
        part = pl.ds(i * rows, rows)
        slots[:, part, :] = jnp.swapaxes(raw[part], 0, 1)

    lane = lax.broadcasted_iota(jnp.int32, (1, TILE), 1)

    def masked(column, count):
        return slots[column] * (lane < count).astype(jnp.float32).astype(jnp.bfloat16)

    left = left_lanes((HALF, TILE))

    def add(a, b, gram):
        pair = a * TILES + b
        same[pair] += jnp.where(left, gram[:HALF], gram[HALF:])
        cross[pair] += jnp.where(left, gram[HALF:], gram[:HALF])

    tile_of = [six[1, k] for k in range(MAXT)]
    sides = [masked(six[0, k], six[2, k]) for k in range(MAXT)]
    for pair in range(MAXT // 2):
        gram = tn_dot(jnp.concatenate(sides[:2 * pair + 2], axis=1), jnp.concatenate(sides[2 * pair:2 * pair + 2], axis=1))
        for b in (2 * pair, 2 * pair + 1):
            for a in range(b + 1):
                block = gram[a * TILE:(a + 1) * TILE, (b - 2 * pair) * TILE:(b - 2 * pair + 1) * TILE]
                add(tile_of[a], tile_of[b], block)
    for j in range(DOUBLES):
        both = jnp.concatenate([masked(twos[0, j], twos[4, j]), masked(twos[1, j], twos[5, j])], axis=1)
        gram = tn_dot(both, both)
        low, high = twos[2, j], twos[3, j]
        add(low, low, gram[:TILE, :TILE])
        add(low, high, gram[:TILE, TILE:])
        add(high, high, gram[TILE:, TILE:])
    for j in range(SINGLES):
        only = masked(ones[0, j], ones[2, j])
        add(ones[1, j], ones[1, j], tn_dot(only, only))

    z = lax.axis_index("batch")
    near = left_lanes((STRIP, TILE))
    row_of = lax.broadcasted_iota(jnp.int32, (HALF, TILE), 0)
    col_of = lax.broadcasted_iota(jnp.int32, (HALF, TILE), 1) & (HALF - 1)
    for a in range(TILES):
        for b in range(a, TILES):
            block = same[a * TILES + b]
            if a == b and a % 2 == 1:
                continue
            if a == b:
                beside = same[(a + 1) * (TILES + 1)]
                block = jnp.where(row_of >= col_of, block, beside)
                diagonal = jnp.sum(jnp.where(row_of == col_of, beside, 0.0), axis=0, keepdims=True)
                for i in range(2):
                    out_ref[legs[(z & 1) * 2 + i] + BLOCKS * STRIP // EIGHT, a // 2:a // 2 + 1, :] = diagonal
            top, bottom = block[:STRIP], block[STRIP:]
            first = jnp.where(near, top, pltpu.roll(bottom, HALF, 1))
            second = jnp.where(near, pltpu.roll(top, HALF, 1), bottom)
            odd = (a ^ b) & 1
            index = same_index(a, b, odd)
            for i, value in enumerate((first, second)):
                to_y = ((z & 1) ^ odd) * 2 + i
                rows = pl.ds(legs[to_y] + index * (STRIP // EIGHT), STRIP // EIGHT)
                out_ref[rows] = value.reshape(STRIP // EIGHT, EIGHT, TILE)
    for k in range(RING):
        target = legs[RING + (k ^ (z >> 1))]
        for index in range(TILES):
            a, b = cross_pair(k, index)
            if a == b:
                value = jnp.where(left, cross[(a + 1) * (TILES + 1)], cross[a * (TILES + 1)])
            else:
                value = cross[a * TILES + b]
            rows = pl.ds(target + index * (HALF // EIGHT), HALF // EIGHT)
            out_ref[rows] = value.reshape(HALF // EIGHT, EIGHT, TILE)


def grams(half_ints, domain_tiles, tile_counts):
    fit_rows = half_ints.shape[0]
    hbm = pl.BlockSpec(memory_space=pltpu.HBM)
    return pl.pallas_call(
        gram_kernel,
        in_specs=[hbm, pl.BlockSpec(memory_space=pl.ANY)],
        out_specs=pl.BlockSpec(memory_space=pltpu.VMEM),
        out_shape=jax.ShapeDtypeStruct((CORES * RING * SHARE // EIGHT, EIGHT, TILE), jnp.float32),
        scratch_shapes=[
            pltpu.VMEM((fit_rows, SLOTS, TILE), jnp.bfloat16),
            pltpu.VMEM((SLOTS, fit_rows, TILE), jnp.bfloat16),
            pltpu.VMEM((TILES * TILES, HALF, TILE), jnp.float32),
            pltpu.VMEM((TILES * TILES, HALF, TILE), jnp.float32),
            pltpu.SMEM((3, ORBITALS), jnp.int32),
            pltpu.SMEM((6, ORBITALS), jnp.int32),
            pltpu.SMEM((3, MAXT), jnp.int32),
            pltpu.SMEM((CORES * RING,), jnp.int32),
            pltpu.SMEM((MAXT, ORBITALS), jnp.int32),
            pltpu.SemaphoreType.DMA((CHUNKS,)),
            pltpu.SemaphoreType.DMA,
        ],
        compiler_params=pltpu.CompilerParams(vmem_limit_bytes=48 * 2**20),
        name="grams",
    )((domain_tiles * 256 + tile_counts).T, half_ints)


def ring_moves(step, turn):
    moves = []
    for x in range(RING):
        for y in range(RING):
            for core in range(CORES):
                along_x = core != turn
                to_x = (x + step) % RING if along_x else x
                to_y = y if along_x else (y + step) % RING
                moves.append(((x * RING + y) * CORES + core, (to_x * RING + to_y) * CORES + core))
    return moves


def expand_kernel(own_ref, one_ref, two_ref, three_ref, out_ref, line, blocks):
    line[...] = own_ref[...] + one_ref[...] + two_ref[...] + three_ref[...]
    x, y, core = place()
    z = lax.axis_index("batch")
    near = left_lanes((STRIP, TILE))

    def pack(pair):
        top, bottom = pair[:STRIP], pair[STRIP:]
        return (
            jnp.where(near, top, pltpu.roll(bottom, HALF, 1)),
            jnp.where(near, pltpu.roll(top, HALF, 1), bottom),
        )

    def keep_flipped(pairs, indices):
        turned = jnp.concatenate(pairs, axis=0).T
        flipped = (*pack(turned[:HALF]), *pack(turned[HALF:]))
        for index, value in zip(indices, flipped):
            blocks[BLOCKS + index] = value

    @pl.when(core == 0)
    def _():
        packed = [line[n * STRIP:(n + 1) * STRIP] for n in range(BLOCKS)]
        for n in range(BLOCKS):
            blocks[n] = packed[n]
        pairs = []
        for n in range(0, BLOCKS, 2):
            a, b = packed[n], packed[n + 1]
            top = jnp.where(near, a, pltpu.roll(b, HALF, 1))
            bottom = jnp.where(near, pltpu.roll(a, HALF, 1), b)
            pairs.append(jnp.concatenate([top, bottom], axis=0))
        for n in range(0, BLOCKS, 4):
            keep_flipped(pairs[n // 2:n // 2 + 2], (n, n + 2, n + 1, n + 3))
        odd = (y >> 1) ^ (z & 1)
        row_of = lax.broadcasted_iota(jnp.int32, (STRIP, TILE), 0)
        lane_of = lax.broadcasted_iota(jnp.int32, (STRIP, TILE), 1)
        row_of = row_of + (lane_of // HALF) * STRIP
        col_of = lane_of & (HALF - 1)
        diagonals = line[BLOCKS * STRIP:]
        on_half = (lax.broadcasted_iota(jnp.int32, (EXTRA, TILE), 1) // HALF) == (y & 1)
        diagonals = jnp.where(on_half, diagonals, pltpu.roll(diagonals, HALF, 1))

        @pl.when(odd == 0)
        def _():
            for m in range(DIAGONALS):
                both, turned = blocks[12 + m], blocks[BLOCKS + 12 + m]
                second = jnp.where(row_of < col_of, both, turned)
                blocks[12 + m] = jnp.where(row_of >= col_of, both, turned)
                blocks[BLOCKS + 12 + m] = jnp.where(row_of == col_of, diagonals[m:m + 1], second)

        for to_x in range(RING):
            for col in range(TILES):
                row = 2 * to_x + ((col & 1) ^ odd)
                index = same_index(jnp.minimum(row, col), jnp.maximum(row, col), odd)
                flip = jnp.where(row == col, (row & 1) == 1, row > col)
                out_ref[((to_x - x) & (RING - 1)) * TILES + col] = blocks[jnp.where(flip, index + BLOCKS, index)]

    @pl.when(core == 1)
    def _():
        pairs = [line[n * HALF:(n + 1) * HALF] for n in range(TILES)]
        for n in range(TILES):
            blocks[2 * n], blocks[2 * n + 1] = pack(pairs[n])
        for n in range(0, TILES, 2):
            keep_flipped(pairs[n:n + 2], (2 * n, 2 * n + 2, 2 * n + 1, 2 * n + 3))
        k = x ^ (z >> 1)
        for to_y in range(RING):
            for col in range(TILES):
                row = 2 * ((col >> 1) ^ k) + (to_y >> 1)
                i = to_y & 1
                low, high = jnp.minimum(row, col), jnp.maximum(row, col)
                m = low >> 1
                index = jnp.where(k == 1, m >> 1, m) * 4 + (low & 1) * 2 + (high & 1)
                index = jnp.where(k == 0, jnp.where(row == col, 4 + m, m), index)
                lower_half = jnp.where(row == col, row & 1, jnp.where(row < col, i, 1 - i))
                direct = jnp.where(row == col, (row & 1) == i, row < col)
                index = index * 2 + 1 - lower_half
                out_ref[((to_y - y) & (RING - 1)) * TILES + col] = blocks[jnp.where(direct, index, index + BLOCKS)]


def expand(*pieces):
    vmem = pl.BlockSpec(memory_space=pltpu.VMEM)
    return pl.pallas_call(
        expand_kernel,
        in_specs=[vmem] * len(pieces),
        out_specs=vmem,
        out_shape=jax.ShapeDtypeStruct((RING * TILES, STRIP, TILE), jnp.float32),
        scratch_shapes=[
            pltpu.VMEM((SHARE, TILE), jnp.float32),
            pltpu.VMEM((2 * BLOCKS, STRIP, TILE), jnp.float32),
        ],
        compiler_params=pltpu.CompilerParams(vmem_limit_bytes=8 * 2**20),
        name="expand",
    )(*pieces)


def last_groups():
    groups = []
    for x in range(RING):
        for odd in range(2):
            for i in range(2):
                groups.append([
                    ((x * RING + ((z & 1) ^ odd) * 2 + i) * CORES) * TILES + z for z in range(TILES)
                ])
    for k in range(RING):
        for y in range(RING):
            groups.append([
                ((((z >> 1) ^ k) * RING + y) * CORES + 1) * TILES + z for z in range(TILES)
            ])
    return groups


def local(half_ints, domain_tiles, tile_counts):
    parts = grams(half_ints, domain_tiles, tile_counts).reshape(CORES, RING, SHARE, TILE)
    keep, send = parts[0], parts[1]
    swap = [(f, f ^ 1) for f in range(RING * RING * CORES)]
    arrived = {u: lax.ppermute(send[u], "fit", swap) for u in (2, 1, 3, 0)}
    chip = {2: keep[2] + arrived[2]}
    for before, u in ((2, 1), (1, 3), (3, 0)):
        chip[before], ready = lax.optimization_barrier((chip[before], arrived[u]))
        chip[u] = keep[u] + ready
    moved = [lax.ppermute(chip[u], "fit", ring_moves(u, 0)) for u in (2, 1, 3)]
    fit = lax.axis_index("fit")
    core = fit & 1
    column_half = ((fit >> 1) & 1) ^ core
    line = expand(chip[0], *moved).reshape(RING, TILES, STRIP, TILE)
    row = line[0]
    for w in (2, 1, 3):
        row = row + lax.ppermute(line[w], "fit", ring_moves(w, 1))
    row, core, column_half = lax.optimization_barrier((row, core, column_half))
    terms = lax.all_to_all(row, ("fit", "batch"), 0, 0, axis_index_groups=last_groups())
    terms, core, column_half = lax.optimization_barrier((terms, core, column_half))
    mine = jnp.sum(terms, axis=0)
    other = lax.ppermute(mine, "fit", swap)
    at = jnp.arange(TILE, dtype=jnp.int32)[None, :] // HALF
    turned_mine, turned_other = (jnp.roll(block, HALF, axis=1) for block in (mine, other))
    return jnp.where(
        at == column_half,
        jnp.where(core == column_half, mine, turned_mine),
        jnp.where(core == column_half, turned_other, other),
    )


def solution(mesh):
    return jax.shard_map(
        local,
        mesh=mesh,
        in_specs=(P("fit", "batch", None), P("batch", None), P("batch", None)),
        out_specs=P("fit", "batch"),
        check_vma=False,
    )
```
